32 devices in a mesh: grp: 2 (over y), pix: 4 (over z), chan: 2 (over x), sub: 2 (over core).
Axes of the slice: x: 2, y: 2, z: 4, core: 2. Of those that a mesh axis runs over, the one named last changes fastest.
Arguments:
- features: bfloat16 [256, 131072], P('chan', ('grp', 'pix', 'sub')), parts along dimension 1, may hold values from -6 to 6
- neighbours: int32 [8, 131072], P(None, ('grp', 'pix', 'sub')), parts along dimension 1, may hold values from 0 to 8703, as said below
- live_cols: int32 [16], P(('grp', 'pix', 'sub')), parts along dimension 0, may hold values from 8 to 32, as said below
- cheb_weight: bfloat16 [7, 256, 256], replicated, may hold values from -0.125 to 0.125
- out_bias: float32 [256], replicated, may hold values from -3 to 3
Outputs:
- mixed: bfloat16 [16, 8192, 256], P(('grp', 'pix', 'sub'), 'chan'), parts along dimension 0
The draws below stay inside these ranges and needn't reach their ends.
There are 2 independent parts, one for each index of `grp`. The reference program is written for one: setup_inputs(seed, part) draws one part's arguments, and reference() takes and returns one part's arrays. A program takes and returns all parts, laid end to end along the dimension named above; an argument that names none is the same for every part. Nothing has to cross between parts.
Inputs may be any that keep to these rules, and one draw needn't show every extreme that they name: `live_cols`: every patch has at least 8 live columns; some patch has all 32 columns live. `neighbours`: entries are extended indices as in the reference program. Entry t of a live slot at column c and latitude l names either the slot itself (extended index 256 + s) or the slot at column c + dc and latitude l + dl, with (dc, dl) = (-1,-1), (-1,0), (-1,1), (0,-1), (0,1), (1,-1), (1,0), (1,1) for t = 0 to 7; column -1 means the last live column of the previous patch and column live_cols[p] the first column of the next patch, and the latitude stays within 0 to 255. Dead slots name only themselves.
All inputs are finite; a program needn't handle non-finite values.
Results may differ from the reference program's by a relative error of at most 0.0039.
Values may be sent and summed in bfloat16 or wider, within the bound.
No kernel may reach another device: no remote copies, remote signals or barrier semaphores. Data moves between devices by JAX's collectives and lax.ppermute only.
A program may use at most 64 MiB of HBM per device.

```python
import jax
import jax.numpy as jnp

CIN = 256
COUT = 256
DEG = 6
LATS = 256
SPAN = 32
ROWS = 8192
DEV_PIX = 8
PIXELS = 65536


def live_columns(key):
    folded = jax.random.fold_in(key, 11)
    key_cols, key_full = jax.random.split(folded)
    columns = jax.random.randint(key_cols, (DEV_PIX,), max(SPAN // 4, DEG), SPAN + 1)
    chosen = jax.random.randint(key_full, (), 0, DEV_PIX)
    columns = jnp.where(jnp.arange(DEV_PIX) == chosen, SPAN, columns)
    return columns.astype(jnp.int32)


def draw_live_cols(key, part):
    return live_columns(key)


def draw_neighbours(key, part):
    columns = live_columns(key)
    slots = jnp.arange(ROWS, dtype=jnp.int32)[None, :]
    column = slots // LATS
    latitude = slots % LATS
    limit = columns[:, None]
    itself = LATS + slots + jnp.zeros((DEV_PIX, 1), jnp.int32)
    alive = column < limit
    offsets = [(-1, -1), (-1, 0), (-1, 1), (0, -1), (0, 1), (1, -1), (1, 0), (1, 1)]
    drops = jax.random.randint(jax.random.fold_in(key, 23), (8, DEV_PIX, ROWS), 0, 16)
    listed = []
    for tap_index in range(8):
        step_col, step_lat = offsets[tap_index]
        new_col = column + step_col
        new_lat = latitude + step_lat
        inside = (new_lat >= 0) & (new_lat < LATS) & alive & (drops[tap_index] != 0)
        extended = jnp.where(new_col < 0, new_lat, jnp.where(new_col >= limit, LATS + ROWS + new_lat, LATS + new_col * LATS + new_lat))
        listed.append(jnp.where(inside, extended, itself))
    return jnp.stack(listed).reshape(8, DEV_PIX * ROWS).astype(jnp.int32)


def steps_of(key, dims, cuts, smallest, top_value):
    factor_of, own = 1.0, jax.random.fold_in(key, 6)
    for position, parts in cuts:
        steps = jnp.exp(jax.random.uniform(jax.random.fold_in(own, position), (parts,), jnp.float32, smallest / len(cuts), top_value / len(cuts)))
        factor_of = factor_of * jnp.repeat(steps, dims[position] // parts).reshape([-1 if axis == position else 1 for axis in range(len(dims))])
    return factor_of


def noise(stream_key, extent, spread, most, shards=(), kind=jnp.bfloat16):
    array = spread * jax.random.normal(stream_key, extent, jnp.float32)
    if shards:
        array = array * steps_of(stream_key, extent, shards, -0.22, 0.18)
    return jnp.clip(array, -most, most).astype(kind)


def setup_inputs(seed: int = 0, part: int = 0) -> dict:
    key_of = jax.random.split(jax.random.key(seed), 6)
    own_keys = jax.random.split(jax.random.fold_in(key_of[5], part), 6)
    features = noise(own_keys[0], (CIN, PIXELS), 1.0, 6.0, ((0, 2), (1, 8)))
    neighbours = draw_neighbours(jax.random.fold_in(jax.random.fold_in(key_of[5], part), 71), part)
    live_cols = draw_live_cols(jax.random.fold_in(jax.random.fold_in(key_of[5], part), 71), part)
    cheb_weight = noise(key_of[3], (DEG + 1, CIN, COUT), ((DEG + 1) * CIN) ** -0.5, 0.125)
    out_bias = noise(key_of[4], (COUT,), 0.5, 3.0, (), jnp.float32)
    return {"features": features, "neighbours": neighbours, "live_cols": live_cols, "cheb_weight": cheb_weight, "out_bias": out_bias}


def global_index(neighbours, live_cols):
    taps = neighbours.reshape(8, DEV_PIX, ROWS).astype(jnp.int32)
    device = jnp.arange(DEV_PIX, dtype=jnp.int32)[None, :, None]
    before = (device - 1) % DEV_PIX
    after = (device + 1) % DEV_PIX
    left_side = before * ROWS + (live_cols[before] - 1) * LATS + taps
    own_side = device * ROWS + taps - LATS
    right_side = after * ROWS + taps - LATS - ROWS
    joined = jnp.where(taps < LATS, left_side, jnp.where(taps < LATS + ROWS, own_side, right_side))
    return joined.reshape(8, DEV_PIX * ROWS).astype(jnp.int32)


def scaled_step(field, index):
    summed = jnp.zeros(field.shape, jnp.float32)
    for tap_index in range(8):
        summed = summed + jnp.take(field, index[tap_index], axis=1)
    return -0.125 * summed


def mix_term(term, weight):
    return jnp.dot(term.T, weight, preferred_element_type=jnp.float32)


def reference(features, neighbours, live_cols, cheb_weight, out_bias):
    index = global_index(neighbours, live_cols)
    older = features.astype(jnp.float32)
    summed = mix_term(features, cheb_weight[0])
    newer = scaled_step(older, index)
    summed = summed + mix_term(newer.astype(jnp.bfloat16), cheb_weight[1])
    for degree in range(2, DEG + 1):
        upcoming = 2.0 * scaled_step(newer, index) - older
        older, newer = newer, upcoming
        summed = summed + mix_term(newer.astype(jnp.bfloat16), cheb_weight[degree])
    slots = jnp.arange(PIXELS, dtype=jnp.int32)
    owner = slots // ROWS
    alive = (slots % ROWS) < live_cols[owner] * LATS
    result = jnp.where(alive[:, None], summed + out_bias[None, :].astype(jnp.float32), 0.0)
    return result.reshape(DEV_PIX, ROWS, COUT).astype(jnp.bfloat16)
```

```python
import functools

import jax
import jax.numpy as jnp
from jax import lax
from jax.experimental import pallas as pl
from jax.experimental.pallas import tpu as pltpu
from jax.sharding import PartitionSpec as P

DEG = 6
LATS = 256
HALF = LATS // 2
TAPS = 8
TAP_ROWS = 16


def shifted(value, axis, steps):
    count = lax.axis_size(axis)
    pairs = [(source, (source + steps) % count) for source in range(count)]
    return lax.ppermute(value, axis, pairs)


def sorting():
    latitude = lax.broadcasted_iota(jnp.int32, (LATS, LATS), 0)
    lane = lax.broadcasted_iota(jnp.int32, (LATS, LATS), 1)
    home = jnp.where(lane < HALF, 2 * lane, 2 * lane - (LATS - 1))
    return (latitude == home).astype(jnp.float32).astype(jnp.bfloat16)


def pack_kernel(columns, features, neighbours, out):
    channels = features.shape[0]
    sort = sorting()
    start = pl.program_id(0) * columns * LATS
    slots = LATS + start + lax.broadcasted_iota(jnp.int32, (TAPS, columns * LATS), 1)
    present = jnp.where(neighbours[...] != slots, 1.0, 0.0).astype(jnp.bfloat16)
    for column in range(columns):
        lanes = slice(column * LATS, (column + 1) * LATS)
        moved = jnp.dot(features[:, lanes], sort, preferred_element_type=jnp.float32)
        out[column, :channels] = moved.astype(jnp.bfloat16)
        taps = jnp.dot(present[:, lanes], sort, preferred_element_type=jnp.float32)
        out[column, channels:] = jnp.concatenate([taps, jnp.zeros_like(taps)], axis=0).astype(jnp.bfloat16)


def pack(features, neighbours):
    channels, slot_count = features.shape
    span = slot_count // LATS
    columns = 4
    rows = channels + TAP_ROWS
    return pl.pallas_call(
        functools.partial(pack_kernel, columns),
        grid=(span // columns,),
        in_specs=[
            pl.BlockSpec((channels, columns * LATS), lambda i: (0, i)),
            pl.BlockSpec((TAPS, columns * LATS), lambda i: (0, i)),
        ],
        out_specs=pl.BlockSpec((columns, rows, LATS), lambda i: (i, 0, 0)),
        out_shape=jax.ShapeDtypeStruct((span, rows, LATS), jnp.bfloat16),
    )(features, neighbours)


def mask_kernel(width, place, interior, left, right, out):
    start = place[0]

    def body(source, target, column, carry):
        tap = source[column, 0:TAPS].astype(jnp.float32) * -0.25
        own = -2.0 - jnp.sum(tap, axis=0, keepdims=True)
        ahead = jnp.concatenate([pltpu.roll(tap[:, :HALF], HALF - 1, 1), tap[:, HALF:]], axis=1)
        behind = jnp.concatenate([tap[:, :HALF], pltpu.roll(tap[:, HALF:], 1, 1)], axis=1)
        for index in range(3):
            for row, part in ((0, ahead), (1, tap), (2, behind)):
                entry = 3 * index + row
                tap_index = entry if entry < 4 else entry - 1
                coefficient = own if entry == 4 else part[tap_index : tap_index + 1]
                out[target + column, entry] = jnp.broadcast_to(coefficient, (8, LATS))
        return carry

    lax.fori_loop(0, DEG, functools.partial(body, left, 0), 0)
    lax.fori_loop(0, width, functools.partial(body, interior, DEG), 0)
    lax.fori_loop(0, DEG, functools.partial(body, right, start), 0)


def divisor(count, limit):
    return max(d for d in range(1, count + 1) if count % d == 0 and d <= max(limit, 1))


def chunk_kernel(width, first, last, place, interior, left, right, masks, weight, *refs):
    if first:
        out, *fields, terms = refs
    elif last:
        acc, bias, out, *fields, terms = refs
    else:
        acc, out, *fields, terms = refs
    channels = interior.shape[1]
    window = width + 2 * DEG
    start = place[0]

    for source, count, target in ((left, DEG, 0), (interior, width, DEG), (right, DEG, start)):

        def load(column, carry):
            value = source[column]
            fields[0][target + column] = value.astype(jnp.float32)
            terms[target + column, 0:channels] = value
            return carry

        lax.fori_loop(0, count, load, 0)

    def combine(mask, at, side, values, source):
        lanes = slice(side * HALF, (side + 1) * HALF)
        other = slice(source * HALF, (source + 1) * HALF)
        return (
            mask[at][:, lanes] * values[0][:, other]
            + mask[3 + at][:, lanes] * values[1][:, other]
            + mask[6 + at][:, lanes] * values[2][:, other]
        )

    for level in range(1, DEG + 1):
        newer, older, upcoming = fields[(level - 1) % 3], fields[(level - 2) % 3], fields[level % 3]
        columns = window - 2 * level
        together = divisor(columns, 52 * 8 // channels)

        def step(index, carry):
            for member in range(together):
                column = level + index * together + member
                mask = [masks[column, entry] for entry in range(9)]
                for base in range(0, channels, 16):
                    halves = []
                    for row in (base, base + 8):
                        rows = slice(row, row + 8)
                        values = [newer[column - 1, rows], newer[column, rows], newer[column + 1, rows]]
                        even = (
                            combine(mask, 1, 0, values, 0)
                            + combine(mask, 2, 0, values, 1)
                            + pltpu.roll(combine(mask, 0, 0, values, 1), 1, 1)
                        )
                        odd = (
                            combine(mask, 1, 1, values, 1)
                            + combine(mask, 0, 1, values, 0)
                            + pltpu.roll(combine(mask, 2, 1, values, 0), HALF - 1, 1)
                        )
                        value = jnp.concatenate([even, odd], axis=1)
                        if level == 1:
                            value = 0.5 * value
                        else:
                            value = value - older[column, rows]
                        if level < DEG:
                            upcoming[column, rows] = value
                        halves.append(value)
                    at = level * channels + base
                    terms[column, at : at + 16] = jnp.concatenate(halves, axis=0).astype(jnp.bfloat16)
            return carry

        lax.fori_loop(0, columns // together, step, 0)

    sort = sorting() if last else None
    pair = divisor(width, 2)

    def mix(index, carry):
        for member in range(pair):
            column = index * pair + member
            product = jnp.dot(weight[...], terms[DEG + column], preferred_element_type=jnp.float32)
            if not first:
                product = product + acc[column]
            if last:
                alive = (column < place[1]).astype(jnp.float32)
                product = ((product + bias[...]) * alive).astype(out.dtype)
                product = lax.dot_general(
                    sort, product, (((1,), (1,)), ((), ())), preferred_element_type=jnp.float32
                ).astype(out.dtype)
            out[column] = product
        return carry

    lax.fori_loop(0, width // pair, mix, 0)


VMEM = pl.BlockSpec(memory_space=pltpu.VMEM)
SMEM = pl.BlockSpec(memory_space=pltpu.SMEM)


def mask_step(width, place, pieces):
    return pl.pallas_call(
        functools.partial(mask_kernel, width),
        out_shape=jax.ShapeDtypeStruct((width + 2 * DEG, 9, 8, LATS), jnp.float32),
        in_specs=[SMEM, VMEM, VMEM, VMEM],
        out_specs=VMEM,
    )(place, *pieces)


def chunk_step(width, place, pieces, masks, weight, acc, bias):
    channels = pieces[0].shape[1]
    outs = weight.shape[0]
    first, last = acc is None, bias is not None
    window = width + 2 * DEG
    operands = [place, *pieces, masks, weight]
    if not first:
        operands.append(acc)
    if last:
        operands.append(bias)
    return pl.pallas_call(
        functools.partial(chunk_kernel, width, first, last),
        out_shape=jax.ShapeDtypeStruct((width, LATS, outs), jnp.bfloat16 if last else jnp.float32),
        in_specs=[SMEM] + [VMEM] * (len(operands) - 1),
        out_specs=VMEM,
        scratch_shapes=[pltpu.VMEM((window, channels, LATS), jnp.float32)] * 3
        + [pltpu.VMEM((window, (DEG + 1) * channels, LATS), jnp.bfloat16)],
        compiler_params=pltpu.CompilerParams(vmem_limit_bytes=48 * 2**20),
    )(*operands)


def pick(options, index):
    chosen = options[0]
    for position in range(1, len(options)):
        chosen = jnp.where(index == position, options[position], chosen)
    return chosen


def splits(native):
    if native % 64:
        return [(0, native)]
    return [(0, native // 2), (native // 2, 3 * native // 4), (3 * native // 4, native)]


def shards(features, neighbours, live_cols, cheb_weight, out_bias):
    native, slot_count = features.shape
    span = slot_count // LATS
    count = lax.axis_size("chan")
    me = lax.axis_index("chan")
    width = span // count
    live = live_cols[0]
    packed = pack(features, neighbours)
    from_prev = shifted(lax.dynamic_slice_in_dim(packed, live - DEG, DEG, axis=0), ("pix", "sub"), 1)
    from_next = shifted(packed[:DEG], ("pix", "sub"), -1)

    def left_of(rows, target):
        options = []
        for position in range(count):
            edge = position * width
            if edge >= DEG:
                options.append(packed[edge - DEG : edge, rows])
            else:
                options.append(jnp.concatenate([from_prev[edge:, rows], packed[:edge, rows]], axis=0))
        return pick(options, target)

    def right_of(rows, target):
        options = []
        for position in range(count):
            edge = (position + 1) * width
            part = packed[edge : edge + DEG, rows]
            options.append(jnp.pad(part, ((0, 2 * DEG - part.shape[0]), (0, 0), (0, 0))))
        base = pick(options, target)
        kept = jnp.clip(live - (target + 1) * width, 0, DEG)
        return lax.dynamic_update_slice_in_dim(base, from_next[:, rows], kept, axis=0)[:DEG]

    def inside_of(rows, target):
        return lax.dynamic_slice_in_dim(packed[:, rows], target * width, width, axis=0)

    def pieces_of(rows, target):
        return inside_of(rows, target), left_of(rows, target), right_of(rows, target)

    live_here = live - me * width
    place = jnp.stack([DEG + jnp.clip(live_here, 0, width), live_here])
    weights = jnp.transpose(cheb_weight, (2, 0, 1))

    blocks = [(0, 0, native, pieces_of(slice(0, native), me))]
    for distance in range(1, count):
        target = lax.rem(me + distance, count)
        for low, high in splits(native):
            sent = pieces_of(slice(low, high), target)
            blocks.append((distance, low, high, tuple(shifted(piece, "chan", distance) for piece in sent)))

    masks = mask_step(width, place, pieces_of(slice(native, native + TAP_ROWS), me))
    acc = None
    for index, (distance, low, high, pieces) in enumerate(blocks):
        source = lax.rem(me - distance + count, count)
        weight = lax.dynamic_slice_in_dim(weights, source * native + low, high - low, axis=2)
        weight = weight.reshape(weights.shape[0], -1)
        bias = out_bias[:, None] if index == len(blocks) - 1 else None
        acc = chunk_step(width, place, pieces, masks, weight, acc, bias)
    return acc.reshape(1, width * LATS, acc.shape[2])


def solution(mesh):
    in_specs = (
        P("chan", ("grp", "pix", "sub")),
        P(None, ("grp", "pix", "sub")),
        P(("grp", "pix", "sub")),
        P(),
        P(),
    )
    out_specs = P(("grp", "pix", "sub"), "chan", None)
    return jax.shard_map(shards, mesh=mesh, in_specs=in_specs, out_specs=out_specs, check_vma=False)
```

```python
import functools

import jax
import jax.numpy as jnp
from jax import lax
from jax.experimental import pallas as pl
from jax.experimental.pallas import tpu as pltpu
from jax.sharding import PartitionSpec as P

DEG = 6
LATS = 256
HALF = LATS // 2
TAPS = 8
TAP_ROWS = 16


def shifted(value, axis, steps):
    count = lax.axis_size(axis)
    pairs = [(source, (source + steps) % count) for source in range(count)]
    return lax.ppermute(value, axis, pairs)


def sorting():
    latitude = lax.broadcasted_iota(jnp.int32, (LATS, LATS), 0)
    lane = lax.broadcasted_iota(jnp.int32, (LATS, LATS), 1)
    home = jnp.where(lane < HALF, 2 * lane, 2 * lane - (LATS - 1))
    return (latitude == home).astype(jnp.float32).astype(jnp.bfloat16)


VMEM = pl.BlockSpec(memory_space=pltpu.VMEM)
SMEM = pl.BlockSpec(memory_space=pltpu.SMEM)
ANY = pl.BlockSpec(memory_space=pl.ANY)


def pack_kernel(span, width, targets, groups, place, features, neighbours, *refs):
    packed, last, first, *early = refs[: 3 + targets]
    held, listed, present, moved, in_sems, out_sems, edge_sems = refs[3 + targets :]
    channels = features.shape[0]
    size = span // groups
    lanes = size * LATS
    lists = pltpu.make_async_copy(neighbours, listed, in_sems.at[groups])
    lists.start()
    loads = []
    for group in range(groups):
        part = pl.ds(group * lanes, lanes)
        loads.append(pltpu.make_async_copy(features.at[:, part], held.at[:, part], in_sems.at[group]))
        loads[-1].start()
    sort = sorting()
    lists.wait()
    slots = LATS + lax.broadcasted_iota(jnp.int32, listed.shape, 1)
    present[0:TAPS] = jnp.where(listed[...] != slots, 1.0, 0.0).astype(jnp.bfloat16)
    present[TAPS:] = jnp.zeros((TAP_ROWS - TAPS, listed.shape[1]), jnp.bfloat16)
    stores = []
    for group in range(groups):
        loads[group].wait()
        for column in range(group * size, (group + 1) * size):
            at = slice(column * LATS, (column + 1) * LATS)
            value = jnp.concatenate([held[:, at], present[:, at]], axis=0)
            moved[column] = jnp.dot(value, sort, preferred_element_type=jnp.float32).astype(jnp.bfloat16)
        part = pl.ds(group * size, size)
        stores.append(pltpu.make_async_copy(moved.at[part], packed.at[part], out_sems.at[group]))
        stores[-1].start()
    for index in range(targets):
        part = moved.at[pl.ds(place[1 + index], width), pl.ds(0, channels)]
        stores.append(pltpu.make_async_copy(part, early[index], edge_sems.at[2 + index]))
    stores.append(pltpu.make_async_copy(moved.at[pl.ds(place[0] - DEG, DEG)], last, edge_sems.at[0]))
    stores.append(pltpu.make_async_copy(moved.at[pl.ds(0, DEG)], first, edge_sems.at[1]))
    for store in stores[groups:]:
        store.start()
    for store in stores:
        store.wait()


def pack(features, neighbours, place, width, targets):
    channels, slot_count = features.shape
    span = slot_count // LATS
    rows = channels + TAP_ROWS
    groups = 4
    shapes = [(span, rows), (DEG, rows), (DEG, rows)] + [(width, channels)] * targets
    return pl.pallas_call(
        functools.partial(pack_kernel, span, width, targets, groups),
        in_specs=[SMEM, ANY, ANY],
        out_specs=[ANY] * len(shapes),
        out_shape=[jax.ShapeDtypeStruct(shape + (LATS,), jnp.bfloat16) for shape in shapes],
        scratch_shapes=[
            pltpu.VMEM(features.shape, jnp.bfloat16),
            pltpu.VMEM(neighbours.shape, jnp.int32),
            pltpu.VMEM((TAP_ROWS, slot_count), jnp.bfloat16),
            pltpu.VMEM((span, rows, LATS), jnp.bfloat16),
            pltpu.SemaphoreType.DMA((groups + 1,)),
            pltpu.SemaphoreType.DMA((groups,)),
            pltpu.SemaphoreType.DMA((2 + targets,)),
        ],
        compiler_params=pltpu.CompilerParams(vmem_limit_bytes=16 * 2**20),
    )(place, features, neighbours)


def over(low, high, body):
    def step(index, carry):
        body(index)
        return carry

    lax.fori_loop(low, jnp.maximum(low, high), step, 0)


def extended(begin, size, live, packed, prev, after, put):
    end = begin + size
    over(begin, jnp.minimum(end, 0), lambda e: put(e - begin, prev, e + DEG))
    over(jnp.maximum(begin, 0), jnp.minimum(end, live), lambda e: put(e - begin, packed, e))
    over(jnp.maximum(begin, live), end, lambda e: put(e - begin, after, jnp.minimum(e - live, DEG - 1)))


def rim_kernel(width, parts, place, packed, prev, after, *rims):
    live, begin = place[0], place[1]

    def copy(offset):
        def put(i, source, column):
            for (low, high), out in zip(parts, rims):
                out[offset + i] = source[column, low:high]

        return put

    extended(begin - DEG, DEG, live, packed, prev, after, copy(0))
    extended(begin + jnp.clip(live - begin, 0, width), DEG, live, packed, prev, after, copy(DEG))


def rims_of(place, packed, prev, after, width, parts):
    shapes = [(2 * DEG, high - low, LATS) for low, high in parts]
    return pl.pallas_call(
        functools.partial(rim_kernel, width, parts),
        in_specs=[SMEM, VMEM, VMEM, VMEM],
        out_specs=[VMEM] * len(shapes),
        out_shape=[jax.ShapeDtypeStruct(shape, jnp.bfloat16) for shape in shapes],
        compiler_params=pltpu.CompilerParams(vmem_limit_bytes=16 * 2**20),
    )(place, packed, prev, after)


def divisor(count, limit):
    return max(d for d in range(1, count + 1) if count % d == 0 and d <= max(limit, 1))


def coefficients(masks, column, value):
    tap = value.astype(jnp.float32)[0:TAPS] * -0.25
    masks[column, 0:8] = jnp.concatenate([pltpu.roll(tap[:, :HALF], HALF - 1, 1), tap[:, HALF:]], axis=1)
    masks[column, 8:16] = tap
    masks[column, 16:24] = jnp.concatenate([tap[:, :HALF], pltpu.roll(tap[:, HALF:], 1, 1)], axis=1)
    own = -2.0 - jnp.sum(tap, axis=0, keepdims=True)
    masks[column, 24:32] = jnp.broadcast_to(own, (8, LATS))


def mask_row(entry):
    index, row = entry // 3, entry % 3
    if entry == 4:
        return 24
    return 8 * row + (entry if entry < 4 else entry - 1)


def chunk_kernel(width, channels, low, last, place, *refs):
    native = low is None
    live, begin, source_channel = place[0], place[1], place[2]
    window = width + 2 * DEG
    refs = list(refs)

    def take(count):
        taken = refs[:count]
        del refs[:count]
        return taken

    if native:
        packed, prev, after, weight, bias, out, masks = take(7)
    else:
        inside, rims, masks, weight, acc, out = take(6)
    *fields, terms, total, held, weight_in, turned, out_sems, sems, column_sems = take(11)
    result = refs[0] if last else total

    rows = pl.ds(pl.multiple_of(source_channel + (0 if native else low), 16), channels)
    weight_copy = pltpu.make_async_copy(weight.at[:, rows], weight_in, sems.at[0])
    if native:

        def fetch(i, source, column):
            pltpu.make_async_copy(source.at[column], held.at[i], column_sems.at[i]).start()

        extended(begin - DEG, window, live, packed, prev, after, fetch)
        weight_copy.start()
    else:
        inside_copy = pltpu.make_async_copy(inside.at[:, pl.ds(low, channels)], held, sems.at[1])
        inside_copy.start()
        weight_copy.start()
        fetch_acc = pltpu.make_async_copy(acc, total, sems.at[2])
        fetch_acc.start()

    def at(column):
        return jnp.clip(column - (DEG - 1), 0, width + 1)

    def load(column, value):
        fields[0][column] = value.astype(jnp.float32)
        terms[at(column), 0:channels] = value

    if native:
        for column in range(window):
            pltpu.make_async_copy(packed.at[0], held.at[column], column_sems.at[column]).wait()
        for column in range(window):
            load(column, held[column, 0:channels])
            coefficients(masks, column, held[column, channels:])
    else:
        for column in range(DEG):
            load(column, rims[column])
        inside_copy.wait()
        for column in range(width):
            load(DEG + column, held[column])
        start = DEG + jnp.clip(live - begin, 0, width)
        for column in range(DEG):
            load(start + column, rims[DEG + column])

    def stencil(level, column):
        newer, older, upcoming = fields[(level - 1) % 3], fields[(level - 2) % 3], fields[level % 3]
        mask = []
        for entry in range(9):
            row = mask_row(entry)
            mask.append(jnp.broadcast_to(masks[column, row : row + 1], (8, LATS)))

        def combine(at, side, values, source):
            lanes = slice(side * HALF, (side + 1) * HALF)
            other = slice(source * HALF, (source + 1) * HALF)
            return (
                mask[at][:, lanes] * values[0][:, other]
                + mask[3 + at][:, lanes] * values[1][:, other]
                + mask[6 + at][:, lanes] * values[2][:, other]
            )

        for base in range(0, channels, 16):
            halves = []
            for row in (base, base + 8):
                rows = slice(row, row + 8)
                values = [newer[column - 1, rows], newer[column, rows], newer[column + 1, rows]]
                even = (
                    combine(1, 0, values, 0) + combine(2, 0, values, 1) + pltpu.roll(combine(0, 0, values, 1), 1, 1)
                )
                odd = (
                    combine(1, 1, values, 1)
                    + combine(0, 1, values, 0)
                    + pltpu.roll(combine(2, 1, values, 0), HALF - 1, 1)
                )
                value = jnp.concatenate([even, odd], axis=1)
                if level == 1:
                    value = 0.5 * value
                else:
                    value = value - older[column, rows]
                if level < DEG:
                    upcoming[column, rows] = value
                halves.append(value)
            place_in = level * channels + base
            terms[at(column), place_in : place_in + 16] = jnp.concatenate(halves, axis=0).astype(jnp.bfloat16)

    def together(level):
        return divisor(window - 2 * level, 52 * 8 // channels)

    for level in range(1, DEG):
        group = together(level)

        def step(index):
            for member in range(group):
                stencil(level, level + index * group + member)

        over(0, (window - 2 * level) // group, step)

    weight_copy.wait()
    turned[...] = weight_in[...].reshape((DEG + 1) * channels, -1).T
    if not native:
        fetch_acc.wait()
    sort = sorting() if last else None

    def send(column):
        return pltpu.make_async_copy(result.at[column], out.at[column], out_sems.at[column])

    def mix(column):
        product = jnp.dot(turned[...], terms[1 + column], preferred_element_type=jnp.float32)
        product = product + (bias[...] if native else total[column])
        if last:
            alive = (begin + column < live).astype(jnp.float32)
            product = (product * alive).astype(jnp.bfloat16)
            product = lax.dot_general(
                sort, product, (((1,), (1,)), ((), ())), preferred_element_type=jnp.float32
            ).astype(jnp.bfloat16)
        result[column] = product

    group = together(DEG)

    def finish(index):
        for member in range(group):
            mix(index * group + member)
        for member in range(group):
            send(index * group + member).start()

    def outermost(index):
        for member in range(group):
            stencil(DEG, DEG + index * group + member)

    outermost(0)

    def both(index):
        outermost(index)
        finish(index - 1)

    over(1, width // group, both)
    finish(width // group - 1)
    for column in range(width):
        send(column).wait()


def chunk_step(place, width, channels, low, last, operands, outs):
    native = low is None
    window = width + 2 * DEG
    out_shape = [jax.ShapeDtypeStruct((width, LATS, outs), jnp.bfloat16 if last else jnp.float32)]
    out_specs = [ANY]
    if native:
        specs = [SMEM, ANY, ANY, ANY, ANY, VMEM]
        out_shape.append(jax.ShapeDtypeStruct((window, 32, LATS), jnp.float32))
        out_specs.append(VMEM)
        held = (window, channels + TAP_ROWS, LATS)
    else:
        specs = [SMEM, ANY, VMEM, VMEM, ANY, ANY]
        held = (width, channels, LATS)
    scratch = [pltpu.VMEM((window, channels, LATS), jnp.float32)] * 3
    scratch.append(pltpu.VMEM((width + 2, (DEG + 1) * channels, LATS), jnp.bfloat16))
    scratch.append(pltpu.VMEM((width, outs, LATS), jnp.float32))
    scratch.append(pltpu.VMEM(held, jnp.bfloat16))
    scratch.append(pltpu.VMEM((DEG + 1, channels, outs), jnp.bfloat16))
    scratch.append(pltpu.VMEM((outs, (DEG + 1) * channels), jnp.bfloat16))
    scratch.append(pltpu.SemaphoreType.DMA((width,)))
    scratch.append(pltpu.SemaphoreType.DMA((3,)))
    scratch.append(pltpu.SemaphoreType.DMA((window,)))
    if last:
        scratch.append(pltpu.VMEM((width, LATS, outs), jnp.bfloat16))
    return pl.pallas_call(
        functools.partial(chunk_kernel, width, channels, low, last),
        out_shape=out_shape,
        in_specs=specs,
        out_specs=out_specs,
        scratch_shapes=scratch,
        compiler_params=pltpu.CompilerParams(vmem_limit_bytes=(40 if native else 28) * 2**20),
    )(place, *operands)


def splits(native):
    if native % 64:
        return [(0, native)]
    return [(0, native // 2), (native // 2, 3 * native // 4), (3 * native // 4, native)]


def shards(features, neighbours, live_cols, cheb_weight, out_bias):
    native, slot_count = features.shape
    outs = cheb_weight.shape[2]
    count = lax.axis_size("chan")
    me = lax.axis_index("chan")
    width = slot_count // LATS // count
    live = live_cols[0]
    parts = splits(native)
    targets = [lax.rem(me + distance, count) * width for distance in range(1, count)]
    packed, last_cols, first_cols, *early = pack(
        features, neighbours, jnp.stack([live] + targets), width, count - 1
    )
    insides = [shifted(early[distance - 1], "chan", distance) for distance in range(1, count)]
    prev = shifted(last_cols, ("pix", "sub"), 1)
    after = shifted(first_cols, ("pix", "sub"), -1)
    blocks = []
    for distance in range(1, count):
        place = jnp.stack([live, targets[distance - 1]])
        rims = rims_of(place, packed, prev, after, width, parts)
        for part, value in zip(parts, rims):
            blocks.append((distance, part, shifted(value, "chan", distance)))

    def place_of(distance):
        source = lax.rem(me - distance + count, count)
        return jnp.stack([live, me * width, source * native])

    bias = jnp.broadcast_to(out_bias[:, None], (outs, LATS))
    acc, masks = chunk_step(
        place_of(0), width, native, None, False, [packed, prev, after, cheb_weight, bias], outs
    )
    for index, (distance, (low, high), rims) in enumerate(blocks):
        operands = [insides[distance - 1], rims, masks, cheb_weight, acc]
        last = index == len(blocks) - 1
        (acc,) = chunk_step(place_of(distance), width, high - low, low, last, operands, outs)
    return acc.reshape(1, width * LATS, acc.shape[2])


def solution(mesh):
    in_specs = (
        P("chan", ("grp", "pix", "sub")),
        P(None, ("grp", "pix", "sub")),
        P(("grp", "pix", "sub")),
        P(),
        P(),
    )
    out_specs = P(("grp", "pix", "sub"), "chan", None)
    return jax.shard_map(shards, mesh=mesh, in_specs=in_specs, out_specs=out_specs, check_vma=False)
```

```python
import functools

import jax
import jax.numpy as jnp
from jax import lax
from jax.experimental import pallas as pl
from jax.experimental.pallas import tpu as pltpu
from jax.sharding import PartitionSpec as P

DEG = 6
LATS = 256
HALF = LATS // 2
TAPS = 8
TAP_ROWS = 16


def shifted(value, axis, steps):
    count = lax.axis_size(axis)
    pairs = [(source, (source + steps) % count) for source in range(count)]
    return lax.ppermute(value, axis, pairs)


def sorting():
    latitude = lax.broadcasted_iota(jnp.int32, (LATS, LATS), 0)
    lane = lax.broadcasted_iota(jnp.int32, (LATS, LATS), 1)
    home = jnp.where(lane < HALF, 2 * lane, 2 * lane - (LATS - 1))
    return (latitude == home).astype(jnp.float32).astype(jnp.bfloat16)


VMEM = pl.BlockSpec(memory_space=pltpu.VMEM)
SMEM = pl.BlockSpec(memory_space=pltpu.SMEM)
ANY = pl.BlockSpec(memory_space=pl.ANY)


def pack_kernel(span, width, targets, groups, place, features, neighbours, *refs):
    packed, last, first, *early = refs[: 3 + targets]
    held, listed, present, moved, in_sems, out_sems, edge_sems = refs[3 + targets :]
    channels = features.shape[0]
    size = span // groups
    lanes = size * LATS
    lists = pltpu.make_async_copy(neighbours, listed, in_sems.at[groups])
    lists.start()
    loads = []
    for group in range(groups):
        part = pl.ds(group * lanes, lanes)
        loads.append(pltpu.make_async_copy(features.at[:, part], held.at[:, part], in_sems.at[group]))
        loads[-1].start()
    sort = sorting()
    lists.wait()
    slots = LATS + lax.broadcasted_iota(jnp.int32, listed.shape, 1)
    present[0:TAPS] = jnp.where(listed[...] != slots, 1.0, 0.0).astype(jnp.bfloat16)
    present[TAPS:] = jnp.zeros((TAP_ROWS - TAPS, listed.shape[1]), jnp.bfloat16)
    stores = []
    for group in range(groups):
        loads[group].wait()
        for column in range(group * size, (group + 1) * size):
            at = slice(column * LATS, (column + 1) * LATS)
            value = jnp.concatenate([held[:, at], present[:, at]], axis=0)
            moved[column] = jnp.dot(value, sort, preferred_element_type=jnp.float32).astype(jnp.bfloat16)
        part = pl.ds(group * size, size)
        stores.append(pltpu.make_async_copy(moved.at[part], packed.at[part], out_sems.at[group]))
        stores[-1].start()
    for index in range(targets):
        part = moved.at[pl.ds(place[1 + index], width), pl.ds(0, channels)]
        stores.append(pltpu.make_async_copy(part, early[index], edge_sems.at[2 + index]))
    stores.append(pltpu.make_async_copy(moved.at[pl.ds(place[0] - DEG, DEG)], last, edge_sems.at[0]))
    stores.append(pltpu.make_async_copy(moved.at[pl.ds(0, DEG)], first, edge_sems.at[1]))
    for store in stores[groups:]:
        store.start()
    for store in stores:
        store.wait()


def pack(features, neighbours, place, width, targets):
    channels, slot_count = features.shape
    span = slot_count // LATS
    rows = channels + TAP_ROWS
    groups = 4
    shapes = [(span, rows), (DEG, rows), (DEG, rows)] + [(width, channels)] * targets
    return pl.pallas_call(
        functools.partial(pack_kernel, span, width, targets, groups),
        in_specs=[SMEM, ANY, ANY],
        out_specs=[ANY] * len(shapes),
        out_shape=[jax.ShapeDtypeStruct(shape + (LATS,), jnp.bfloat16) for shape in shapes],
        scratch_shapes=[
            pltpu.VMEM(features.shape, jnp.bfloat16),
            pltpu.VMEM(neighbours.shape, jnp.int32),
            pltpu.VMEM((TAP_ROWS, slot_count), jnp.bfloat16),
            pltpu.VMEM((span, rows, LATS), jnp.bfloat16),
            pltpu.SemaphoreType.DMA((groups + 1,)),
            pltpu.SemaphoreType.DMA((groups,)),
            pltpu.SemaphoreType.DMA((2 + targets,)),
        ],
        compiler_params=pltpu.CompilerParams(vmem_limit_bytes=16 * 2**20),
    )(place, features, neighbours)


def over(low, high, body):
    def step(index, carry):
        body(index)
        return carry

    lax.fori_loop(low, jnp.maximum(low, high), step, 0)


def extended(begin, size, live, packed, prev, after, put):
    end = begin + size
    over(begin, jnp.minimum(end, 0), lambda e: put(e - begin, prev, e + DEG))
    over(jnp.maximum(begin, 0), jnp.minimum(end, live), lambda e: put(e - begin, packed, e))
    over(jnp.maximum(begin, live), end, lambda e: put(e - begin, after, jnp.minimum(e - live, DEG - 1)))


def rim_kernel(width, parts, place, packed, prev, after, *rims):
    live, begin = place[0], place[1]

    def copy(offset):
        def put(i, source, column):
            for (low, high), out in zip(parts, rims):
                out[offset + i] = source[column, low:high]

        return put

    extended(begin - DEG, DEG, live, packed, prev, after, copy(0))
    extended(begin + jnp.clip(live - begin, 0, width), DEG, live, packed, prev, after, copy(DEG))


def rims_of(place, packed, prev, after, width, parts):
    shapes = [(2 * DEG, high - low, LATS) for low, high in parts]
    return pl.pallas_call(
        functools.partial(rim_kernel, width, parts),
        in_specs=[SMEM, VMEM, VMEM, VMEM],
        out_specs=[VMEM] * len(shapes),
        out_shape=[jax.ShapeDtypeStruct(shape, jnp.bfloat16) for shape in shapes],
        compiler_params=pltpu.CompilerParams(vmem_limit_bytes=16 * 2**20),
    )(place, packed, prev, after)


def divisor(count, limit):
    return max(d for d in range(1, count + 1) if count % d == 0 and d <= max(limit, 1))


def coefficients(masks, column, value):
    tap = value.astype(jnp.float32)[0:TAPS] * -0.25
    masks[column, 0:8] = jnp.concatenate([pltpu.roll(tap[:, :HALF], HALF - 1, 1), tap[:, HALF:]], axis=1)
    masks[column, 8:16] = tap
    masks[column, 16:24] = jnp.concatenate([tap[:, :HALF], pltpu.roll(tap[:, HALF:], 1, 1)], axis=1)
    own = -2.0 - jnp.sum(tap, axis=0, keepdims=True)
    masks[column, 24:32] = jnp.broadcast_to(own, (8, LATS))


def mask_row(entry):
    index, row = entry // 3, entry % 3
    if entry == 4:
        return 24
    return 8 * row + (entry if entry < 4 else entry - 1)


def chunk_kernel(width, channels, low, last, place, *refs):
    native = low is None
    live, begin, source_channel = place[0], place[1], place[2]
    window = width + 2 * DEG
    refs = list(refs)

    def take(count):
        taken = refs[:count]
        del refs[:count]
        return taken

    if native:
        packed, prev, after, weight, bias, out, masks = take(7)
    else:
        inside, rims, masks, weight, acc, out = take(6)
    *fields, terms, total, held, weight_in, turned, out_sems, sems, column_sems = take(11)
    result = refs[0] if last else total

    rows = pl.ds(pl.multiple_of(source_channel + (0 if native else low), 16), channels)
    weight_copy = pltpu.make_async_copy(weight.at[:, rows], weight_in, sems.at[0])
    if native:

        def fetch(i, source, column):
            pltpu.make_async_copy(source.at[column], held.at[i], column_sems.at[i]).start()

        extended(begin - DEG, window, live, packed, prev, after, fetch)
        weight_copy.start()
    else:
        inside_copy = pltpu.make_async_copy(inside.at[:, pl.ds(low, channels)], held, sems.at[1])
        inside_copy.start()
        weight_copy.start()
        fetch_acc = pltpu.make_async_copy(acc, total, sems.at[2])
        fetch_acc.start()

    def at(column):
        return jnp.clip(column - (DEG - 1), 0, width + 1)

    def load(column, value):
        fields[0][column] = value.astype(jnp.float32)
        terms[at(column), 0:channels] = value

    if native:
        for column in range(window):
            pltpu.make_async_copy(packed.at[0], held.at[column], column_sems.at[column]).wait()
        for column in range(window):
            load(column, held[column, 0:channels])
            coefficients(masks, column, held[column, channels:])
    else:
        for column in range(DEG):
            load(column, rims[column])
        inside_copy.wait()
        for column in range(width):
            load(DEG + column, held[column])
        start = DEG + jnp.clip(live - begin, 0, width)
        for column in range(DEG):
            load(start + column, rims[DEG + column])

    def stencil(level, column):
        newer, older, upcoming = fields[(level - 1) % 3], fields[(level - 2) % 3], fields[level % 3]
        mask = []
        for entry in range(9):
            row = mask_row(entry)
            mask.append(jnp.broadcast_to(masks[column, row : row + 1], (8, LATS)))

        def combine(at, side, values, source):
            lanes = slice(side * HALF, (side + 1) * HALF)
            other = slice(source * HALF, (source + 1) * HALF)
            return (
                mask[at][:, lanes] * values[0][:, other]
                + mask[3 + at][:, lanes] * values[1][:, other]
                + mask[6 + at][:, lanes] * values[2][:, other]
            )

        for base in range(0, channels, 16):
            halves = []
            for row in (base, base + 8):
                rows = slice(row, row + 8)
                values = [newer[column - 1, rows], newer[column, rows], newer[column + 1, rows]]
                even = (
                    combine(1, 0, values, 0) + combine(2, 0, values, 1) + pltpu.roll(combine(0, 0, values, 1), 1, 1)
                )
                odd = (
                    combine(1, 1, values, 1)
                    + combine(0, 1, values, 0)
                    + pltpu.roll(combine(2, 1, values, 0), HALF - 1, 1)
                )
                value = jnp.concatenate([even, odd], axis=1)
                if level == 1:
                    value = 0.5 * value
                else:
                    value = value - older[column, rows]
                if level < DEG:
                    upcoming[column, rows] = value
                halves.append(value)
            place_in = level * channels + base
            terms[at(column), place_in : place_in + 16] = jnp.concatenate(halves, axis=0).astype(jnp.bfloat16)

    def together(level):
        return divisor(window - 2 * level, max(4, 416 // channels))

    for level in range(1, DEG):
        group = together(level)

        def step(index):
            for member in range(group):
                stencil(level, level + index * group + member)

        over(0, (window - 2 * level) // group, step)

    weight_copy.wait()
    turned[...] = weight_in[...].reshape((DEG + 1) * channels, -1).T
    if not native:
        fetch_acc.wait()
    sort = sorting() if last else None

    def send(column):
        return pltpu.make_async_copy(result.at[column], out.at[column], out_sems.at[column])

    def mix(column):
        product = jnp.dot(turned[...], terms[1 + column], preferred_element_type=jnp.float32)
        product = product + (bias[...] if native else total[column])
        if last:
            alive = (begin + column < live).astype(jnp.float32)
            product = (product * alive).astype(jnp.bfloat16)
            product = lax.dot_general(
                sort, product, (((1,), (1,)), ((), ())), preferred_element_type=jnp.float32
            ).astype(jnp.bfloat16)
        result[column] = product

    group = together(DEG)

    def finish(index):
        for member in range(group):
            mix(index * group + member)
        for member in range(group):
            send(index * group + member).start()

    def outermost(index):
        for member in range(group):
            stencil(DEG, DEG + index * group + member)

    outermost(0)

    def both(index):
        outermost(index)
        finish(index - 1)

    over(1, width // group, both)
    finish(width // group - 1)
    for column in range(width):
        send(column).wait()


def chunk_step(place, width, channels, low, last, operands, outs):
    native = low is None
    window = width + 2 * DEG
    out_shape = [jax.ShapeDtypeStruct((width, LATS, outs), jnp.bfloat16 if last else jnp.float32)]
    out_specs = [ANY]
    if native:
        specs = [SMEM, ANY, ANY, ANY, ANY, VMEM]
        out_shape.append(jax.ShapeDtypeStruct((window, 32, LATS), jnp.float32))
        out_specs.append(VMEM)
        held = (window, channels + TAP_ROWS, LATS)
    else:
        specs = [SMEM, ANY, VMEM, VMEM, ANY, ANY]
        held = (width, channels, LATS)
    scratch = [pltpu.VMEM((window, channels, LATS), jnp.float32)] * 3
    scratch.append(pltpu.VMEM((width + 2, (DEG + 1) * channels, LATS), jnp.bfloat16))
    scratch.append(pltpu.VMEM((width, outs, LATS), jnp.float32))
    scratch.append(pltpu.VMEM(held, jnp.bfloat16))
    scratch.append(pltpu.VMEM((DEG + 1, channels, outs), jnp.bfloat16))
    scratch.append(pltpu.VMEM((outs, (DEG + 1) * channels), jnp.bfloat16))
    scratch.append(pltpu.SemaphoreType.DMA((width,)))
    scratch.append(pltpu.SemaphoreType.DMA((3,)))
    scratch.append(pltpu.SemaphoreType.DMA((window,)))
    if last:
        scratch.append(pltpu.VMEM((width, LATS, outs), jnp.bfloat16))
    return pl.pallas_call(
        functools.partial(chunk_kernel, width, channels, low, last),
        out_shape=out_shape,
        in_specs=specs,
        out_specs=out_specs,
        scratch_shapes=scratch,
        compiler_params=pltpu.CompilerParams(vmem_limit_bytes=40 * 2**20),
    )(place, *operands)


def splits(native):
    if native % 64:
        return [(0, native)]
    return [(0, native // 2), (native // 2, 3 * native // 4), (3 * native // 4, native)]


def shards(features, neighbours, live_cols, cheb_weight, out_bias):
    native, slot_count = features.shape
    outs = cheb_weight.shape[2]
    count = lax.axis_size("chan")
    me = lax.axis_index("chan")
    width = slot_count // LATS // count
    live = live_cols[0]
    parts = splits(native)
    targets = [lax.rem(me + distance, count) * width for distance in range(1, count)]
    packed, last_cols, first_cols, *early = pack(
        features, neighbours, jnp.stack([live] + targets), width, count - 1
    )
    insides = [shifted(early[distance - 1], "chan", distance) for distance in range(1, count)]
    prev = shifted(last_cols, ("pix", "sub"), 1)
    after = shifted(first_cols, ("pix", "sub"), -1)
    blocks = []
    for distance in range(1, count):
        place = jnp.stack([live, targets[distance - 1]])
        rims = rims_of(place, packed, prev, after, width, parts)
        for part, value in zip(parts, rims):
            blocks.append((distance, part, shifted(value, "chan", distance)))

    def place_of(distance):
        source = lax.rem(me - distance + count, count)
        return jnp.stack([live, me * width, source * native])

    bias = jnp.broadcast_to(out_bias[:, None], (outs, LATS))
    acc, masks = chunk_step(
        place_of(0), width, native, None, False, [packed, prev, after, cheb_weight, bias], outs
    )
    for index, (distance, (low, high), rims) in enumerate(blocks):
        operands = [insides[distance - 1], rims, masks, cheb_weight, acc]
        last = index == len(blocks) - 1
        (acc,) = chunk_step(place_of(distance), width, high - low, low, last, operands, outs)
    return acc.reshape(1, width * LATS, acc.shape[2])


def solution(mesh):
    in_specs = (
        P("chan", ("grp", "pix", "sub")),
        P(None, ("grp", "pix", "sub")),
        P(("grp", "pix", "sub")),
        P(),
        P(),
    )
    out_specs = P(("grp", "pix", "sub"), "chan", None)
    return jax.shard_map(shards, mesh=mesh, in_specs=in_specs, out_specs=out_specs, check_vma=False)
```

```python
import functools

import jax
import jax.numpy as jnp
from jax import lax
from jax.experimental import pallas as pl
from jax.experimental.pallas import tpu as pltpu
from jax.sharding import PartitionSpec as P

DEG = 6
LATS = 256
HALF = LATS // 2
TAPS = 8
TAP_ROWS = 16


def shifted(value, axis, steps):
    count = lax.axis_size(axis)
    pairs = [(source, (source + steps) % count) for source in range(count)]
    return lax.ppermute(value, axis, pairs)


def sorting():
    latitude = lax.broadcasted_iota(jnp.int32, (LATS, LATS), 0)
    lane = lax.broadcasted_iota(jnp.int32, (LATS, LATS), 1)
    home = jnp.where(lane < HALF, 2 * lane, 2 * lane - (LATS - 1))
    return (latitude == home).astype(jnp.float32).astype(jnp.bfloat16)


VMEM = pl.BlockSpec(memory_space=pltpu.VMEM)
SMEM = pl.BlockSpec(memory_space=pltpu.SMEM)
ANY = pl.BlockSpec(memory_space=pl.ANY)


def pack_kernel(span, width, targets, groups, place, features, neighbours, *refs):
    packed, last, first, *early = refs[: 3 + targets]
    present, moved, out_sems, edge_sems = refs[3 + targets :]
    channels = features.shape[0]
    size = span // groups
    sort = sorting()
    slots = LATS + lax.broadcasted_iota(jnp.int32, neighbours.shape, 1)
    present[0:TAPS] = jnp.where(neighbours[...] != slots, 1.0, 0.0).astype(jnp.bfloat16)
    present[TAPS:] = jnp.zeros((TAP_ROWS - TAPS, neighbours.shape[1]), jnp.bfloat16)
    stores = []
    for group in range(groups):
        for column in range(group * size, (group + 1) * size):
            at = slice(column * LATS, (column + 1) * LATS)
            value = jnp.concatenate([features[:, at], present[:, at]], axis=0)
            moved[column] = jnp.dot(value, sort, preferred_element_type=jnp.float32).astype(jnp.bfloat16)
        part = pl.ds(group * size, size)
        stores.append(pltpu.make_async_copy(moved.at[part], packed.at[part], out_sems.at[group]))
        stores[-1].start()
    for index in range(targets):
        part = moved.at[pl.ds(place[1 + index], width), pl.ds(0, channels)]
        stores.append(pltpu.make_async_copy(part, early[index], edge_sems.at[2 + index]))
    stores.append(pltpu.make_async_copy(moved.at[pl.ds(place[0] - DEG, DEG)], last, edge_sems.at[0]))
    stores.append(pltpu.make_async_copy(moved.at[pl.ds(0, DEG)], first, edge_sems.at[1]))
    for store in stores[groups:]:
        store.start()
    for store in stores:
        store.wait()


def pack(features, neighbours, place, width, targets):
    channels, slot_count = features.shape
    span = slot_count // LATS
    rows = channels + TAP_ROWS
    groups = 4
    shapes = [(span, rows), (DEG, rows), (DEG, rows)] + [(width, channels)] * targets
    return pl.pallas_call(
        functools.partial(pack_kernel, span, width, targets, groups),
        in_specs=[SMEM, VMEM, VMEM],
        out_specs=[ANY] * len(shapes),
        out_shape=[jax.ShapeDtypeStruct(shape + (LATS,), jnp.bfloat16) for shape in shapes],
        scratch_shapes=[
            pltpu.VMEM((TAP_ROWS, slot_count), jnp.bfloat16),
            pltpu.VMEM((span, rows, LATS), jnp.bfloat16),
            pltpu.SemaphoreType.DMA((groups,)),
            pltpu.SemaphoreType.DMA((2 + targets,)),
        ],
        compiler_params=pltpu.CompilerParams(vmem_limit_bytes=16 * 2**20),
    )(place, features, neighbours)


def over(low, high, body):
    def step(index, carry):
        body(index)
        return carry

    lax.fori_loop(low, jnp.maximum(low, high), step, 0)


def extended(begin, size, live, packed, prev, after, put):
    end = begin + size
    over(begin, jnp.minimum(end, 0), lambda e: put(e - begin, prev, e + DEG))
    over(jnp.maximum(begin, 0), jnp.minimum(end, live), lambda e: put(e - begin, packed, e))
    over(jnp.maximum(begin, live), end, lambda e: put(e - begin, after, jnp.minimum(e - live, DEG - 1)))


def rim_kernel(width, parts, place, packed, prev, after, *rims):
    live, begin = place[0], place[1]

    def copy(offset):
        def put(i, source, column):
            for (low, high), out in zip(parts, rims):
                out[offset + i] = source[column, low:high]

        return put

    extended(begin - DEG, DEG, live, packed, prev, after, copy(0))
    extended(begin + jnp.clip(live - begin, 0, width), DEG, live, packed, prev, after, copy(DEG))


def rims_of(place, packed, prev, after, width, parts):
    shapes = [(2 * DEG, high - low, LATS) for low, high in parts]
    return pl.pallas_call(
        functools.partial(rim_kernel, width, parts),
        in_specs=[SMEM, VMEM, VMEM, VMEM],
        out_specs=[VMEM] * len(shapes),
        out_shape=[jax.ShapeDtypeStruct(shape, jnp.bfloat16) for shape in shapes],
        compiler_params=pltpu.CompilerParams(vmem_limit_bytes=16 * 2**20),
    )(place, packed, prev, after)


def divisor(count, limit):
    return max(d for d in range(1, count + 1) if count % d == 0 and d <= max(limit, 1))


def coefficients(masks, column, value):
    tap = value.astype(jnp.float32)[0:TAPS] * -0.25
    masks[column, 0:8] = jnp.concatenate([pltpu.roll(tap[:, :HALF], HALF - 1, 1), tap[:, HALF:]], axis=1)
    masks[column, 8:16] = tap
    masks[column, 16:24] = jnp.concatenate([tap[:, :HALF], pltpu.roll(tap[:, HALF:], 1, 1)], axis=1)
    own = -2.0 - jnp.sum(tap, axis=0, keepdims=True)
    masks[column, 24:32] = jnp.broadcast_to(own, (8, LATS))


def mask_row(entry):
    index, row = entry // 3, entry % 3
    if entry == 4:
        return 24
    return 8 * row + (entry if entry < 4 else entry - 1)


def chunk_kernel(width, channels, low, last, place, *refs):
    native = low is None
    live, begin, source_channel = place[0], place[1], place[2]
    window = width + 2 * DEG
    refs = list(refs)

    def take(count):
        taken = refs[:count]
        del refs[:count]
        return taken

    if native:
        packed, prev, after, weight, bias, out, masks = take(7)
    else:
        inside, rims, masks, weight, acc, out = take(6)
    *fields, terms, total, held, weight_in, turned, out_sems, sems, column_sems = take(11)
    result = refs[0] if last else total

    rows = pl.ds(pl.multiple_of(source_channel + (0 if native else low), 16), channels)
    weight_copy = pltpu.make_async_copy(weight.at[:, rows], weight_in, sems.at[0])
    if native:

        def fetch(i, source, column):
            pltpu.make_async_copy(source.at[column], held.at[i], column_sems.at[i]).start()

        extended(begin - DEG, window, live, packed, prev, after, fetch)
        weight_copy.start()
    else:
        inside_copy = pltpu.make_async_copy(inside.at[:, pl.ds(low, channels)], held, sems.at[1])
        inside_copy.start()
        weight_copy.start()
        fetch_acc = pltpu.make_async_copy(acc, total, sems.at[2])
        fetch_acc.start()

    def at(column):
        return jnp.clip(column - (DEG - 1), 0, width + 1)

    def load(column, value):
        fields[0][column] = value.astype(jnp.float32)
        terms[at(column), 0:channels] = value

    if native:
        for column in range(window):
            pltpu.make_async_copy(packed.at[0], held.at[column], column_sems.at[column]).wait()
        for column in range(window):
            load(column, held[column, 0:channels])
            coefficients(masks, column, held[column, channels:])
    else:
        for column in range(DEG):
            load(column, rims[column])
        inside_copy.wait()
        for column in range(width):
            load(DEG + column, held[column])
        start = DEG + jnp.clip(live - begin, 0, width)
        for column in range(DEG):
            load(start + column, rims[DEG + column])

    def stencil(level, column):
        newer, older, upcoming = fields[(level - 1) % 3], fields[(level - 2) % 3], fields[level % 3]
        mask = []
        for entry in range(9):
            row = mask_row(entry)
            mask.append(jnp.broadcast_to(masks[column, row : row + 1], (8, LATS)))

        def combine(at, side, values, source):
            lanes = slice(side * HALF, (side + 1) * HALF)
            other = slice(source * HALF, (source + 1) * HALF)
            return (
                mask[at][:, lanes] * values[0][:, other]
                + mask[3 + at][:, lanes] * values[1][:, other]
                + mask[6 + at][:, lanes] * values[2][:, other]
            )

        for base in range(0, channels, 16):
            halves = []
            for row in (base, base + 8):
                rows = slice(row, row + 8)
                values = [newer[column - 1, rows], newer[column, rows], newer[column + 1, rows]]
                even = (
                    combine(1, 0, values, 0) + combine(2, 0, values, 1) + pltpu.roll(combine(0, 0, values, 1), 1, 1)
                )
                odd = (
                    combine(1, 1, values, 1)
                    + combine(0, 1, values, 0)
                    + pltpu.roll(combine(2, 1, values, 0), HALF - 1, 1)
                )
                value = jnp.concatenate([even, odd], axis=1)
                if level == 1:
                    value = 0.5 * value
                else:
                    value = value - older[column, rows]
                if level < DEG:
                    upcoming[column, rows] = value
                halves.append(value)
            place_in = level * channels + base
            terms[at(column), place_in : place_in + 16] = jnp.concatenate(halves, axis=0).astype(jnp.bfloat16)

    def together(level):
        return divisor(window - 2 * level, max(4, 416 // channels))

    for level in range(1, DEG):
        group = together(level)

        def step(index):
            for member in range(group):
                stencil(level, level + index * group + member)

        over(0, (window - 2 * level) // group, step)

    weight_copy.wait()
    turned[...] = weight_in[...].reshape((DEG + 1) * channels, -1).T
    if not native:
        fetch_acc.wait()
    sort = sorting() if last else None

    def send(column):
        return pltpu.make_async_copy(result.at[column], out.at[column], out_sems.at[column])

    def mix(column):
        product = jnp.dot(turned[...], terms[1 + column], preferred_element_type=jnp.float32)
        product = product + (bias[...] if native else total[column])
        if last:
            alive = (begin + column < live).astype(jnp.float32)
            product = (product * alive).astype(jnp.bfloat16)
            product = lax.dot_general(
                sort, product, (((1,), (1,)), ((), ())), preferred_element_type=jnp.float32
            ).astype(jnp.bfloat16)
        result[column] = product

    group = together(DEG)

    def finish(index):
        for member in range(group):
            mix(index * group + member)
        for member in range(group):
            send(index * group + member).start()

    def outermost(index):
        for member in range(group):
            stencil(DEG, DEG + index * group + member)

    outermost(0)

    def both(index):
        outermost(index)
        finish(index - 1)

    over(1, width // group, both)
    finish(width // group - 1)
    for column in range(width):
        send(column).wait()


def chunk_step(place, width, channels, low, last, operands, outs):
    native = low is None
    window = width + 2 * DEG
    out_shape = [jax.ShapeDtypeStruct((width, LATS, outs), jnp.bfloat16 if last else jnp.float32)]
    out_specs = [ANY]
    if native:
        specs = [SMEM, ANY, ANY, ANY, ANY, VMEM]
        out_shape.append(jax.ShapeDtypeStruct((window, 32, LATS), jnp.float32))
        out_specs.append(VMEM)
        held = (window, channels + TAP_ROWS, LATS)
    else:
        specs = [SMEM, ANY, VMEM, VMEM, ANY, ANY]
        held = (width, channels, LATS)
    scratch = [pltpu.VMEM((window, channels, LATS), jnp.float32)] * 3
    scratch.append(pltpu.VMEM((width + 2, (DEG + 1) * channels, LATS), jnp.bfloat16))
    scratch.append(pltpu.VMEM((width, outs, LATS), jnp.float32))
    scratch.append(pltpu.VMEM(held, jnp.bfloat16))
    scratch.append(pltpu.VMEM((DEG + 1, channels, outs), jnp.bfloat16))
    scratch.append(pltpu.VMEM((outs, (DEG + 1) * channels), jnp.bfloat16))
    scratch.append(pltpu.SemaphoreType.DMA((width,)))
    scratch.append(pltpu.SemaphoreType.DMA((3,)))
    scratch.append(pltpu.SemaphoreType.DMA((window,)))
    if last:
        scratch.append(pltpu.VMEM((width, LATS, outs), jnp.bfloat16))
    return pl.pallas_call(
        functools.partial(chunk_kernel, width, channels, low, last),
        out_shape=out_shape,
        in_specs=specs,
        out_specs=out_specs,
        scratch_shapes=scratch,
        compiler_params=pltpu.CompilerParams(vmem_limit_bytes=40 * 2**20),
    )(place, *operands)


def splits(native):
    if native % 64:
        return [(0, native)]
    return [(0, native // 2), (native // 2, 3 * native // 4), (3 * native // 4, native)]


def shards(features, neighbours, live_cols, cheb_weight, out_bias):
    native, slot_count = features.shape
    outs = cheb_weight.shape[2]
    count = lax.axis_size("chan")
    me = lax.axis_index("chan")
    width = slot_count // LATS // count
    live = live_cols[0]
    parts = splits(native)
    targets = [lax.rem(me + distance, count) * width for distance in range(1, count)]
    packed, last_cols, first_cols, *early = pack(
        features, neighbours, jnp.stack([live] + targets), width, count - 1
    )
    insides = [shifted(early[distance - 1], "chan", distance) for distance in range(1, count)]
    prev = shifted(last_cols, ("pix", "sub"), 1)
    after = shifted(first_cols, ("pix", "sub"), -1)
    blocks = []
    for distance in range(1, count):
        place = jnp.stack([live, targets[distance - 1]])
        rims = rims_of(place, packed, prev, after, width, parts)
        for part, value in zip(parts, rims):
            blocks.append((distance, part, shifted(value, "chan", distance)))

    def place_of(distance):
        source = lax.rem(me - distance + count, count)
        return jnp.stack([live, me * width, source * native])

    bias = jnp.broadcast_to(out_bias[:, None], (outs, LATS))
    acc, masks = chunk_step(
        place_of(0), width, native, None, False, [packed, prev, after, cheb_weight, bias], outs
    )
    for index, (distance, (low, high), rims) in enumerate(blocks):
        operands = [insides[distance - 1], rims, masks, cheb_weight, acc]
        last = index == len(blocks) - 1
        (acc,) = chunk_step(place_of(distance), width, high - low, low, last, operands, outs)
    return acc.reshape(1, width * LATS, acc.shape[2])


def solution(mesh):
    in_specs = (
        P("chan", ("grp", "pix", "sub")),
        P(None, ("grp", "pix", "sub")),
        P(("grp", "pix", "sub")),
        P(),
        P(),
    )
    out_specs = P(("grp", "pix", "sub"), "chan", None)
    return jax.shard_map(shards, mesh=mesh, in_specs=in_specs, out_specs=out_specs, check_vma=False)
```
